32 devices in a mesh: section: 4 (over z), dp: 4 (over y, x), tensor: 2 (over core).
Axes of the slice: x: 2, y: 2, z: 4, core: 2. Of those that a mesh axis runs over, the one named last changes fastest.
Arguments:
- inputs: bfloat16 [2, 512, 768], P(None, 'dp'), may hold values from -6 to 6
- out_grads: bfloat16 [2, 512, 768], P(None, 'dp'), may hold values from -6 to 6
- norm_gain: float32 [4, 768], P('section'), may hold values from 0.1 to 1.9
- up_weight: bfloat16 [4, 768, 3072], P('section', None, 'tensor'), may hold values from -0.21875 to 0.21875
- down_weight: bfloat16 [4, 3072, 768], P('section', 'tensor'), may hold values from -0.109375 to 0.109375
- prior_up_grad: bfloat16 [4, 4, 768, 3072], P('dp', 'section', None, 'tensor'), may hold values from -6 to 6
- prior_down_grad: bfloat16 [4, 4, 3072, 768], P('dp', 'section', 'tensor'), may hold values from -6 to 6
- master_up: float32 [4, 768, 3072], P('section', 'dp', 'tensor'), may hold values from -0.3 to 0.3
- master_down: float32 [4, 3072, 768], P('section', ('tensor', 'dp')), may hold values from -0.3 to 0.3
Outputs:
- layer_outputs: bfloat16 [4, 2, 512, 768], P('section', None, 'dp')
- input_grads: bfloat16 [4, 2, 512, 768], P('section', None, 'dp')
- new_up: float32 [4, 768, 3072], P('section', 'dp', 'tensor')
- new_down: float32 [4, 3072, 768], P('section', ('tensor', 'dp'))
The draws below stay inside these ranges and needn't reach their ends.
All inputs are finite; a program needn't handle non-finite values.
Results may differ from the reference program's by a relative error of at most 0.019.
Values may be sent and summed in bfloat16 or wider, within the bound.
A program may use at most 128 MiB of HBM per device.

```python
import jax
import jax.numpy as jnp
from jax import lax

D = 768
FF = 3072
MICRO = 2
LAYERS = 4
TOKENS = 512
N_DP = 4


def strengthened(result, stream_key, source, target, parts, factor):
    def block_of(position):
        return (jnp.arange(result.shape[position]) // (result.shape[position] // parts)).reshape((-1,) + (1,) * (result.ndim - 1 - position))

    one_side = jax.random.permutation(stream_key, parts)[block_of(target)]
    other_side = (block_of(target) + parts // 2) % parts
    return jnp.where((block_of(source) == one_side) | (block_of(source) == other_side), factor * result, result)


def block_scale(rng, shape, shards, low, top_value):
    def one(position, shards_of):
        draws = jax.random.uniform(jax.random.fold_in(jax.random.fold_in(rng, 6), position), (shards_of,), jnp.float32, low / len(shards), top_value / len(shards))
        return jnp.repeat(jnp.exp(draws), shape[position] // shards_of).reshape((-1,) + (1,) * (len(shape) - position - 1))

    factor_of = one(*shards[0])
    for cut in shards[1:]:
        factor_of = factor_of * one(*cut)
    return factor_of


def centred(stream_key, dims, scale, most, pieces=(), dtype=jnp.bfloat16):
    loudness = block_scale(stream_key, dims, pieces, -0.22, 0.18) if pieces else 1.0
    drawn = jax.random.normal(stream_key, dims, jnp.float32) * scale * loudness
    return jnp.minimum(jnp.maximum(drawn, -most), most).astype(dtype)


def heavy_noise(rng, dims, scale, most, split, heavy, held_as=jnp.bfloat16):
    drawn = scale * jax.random.normal(rng, dims, jnp.float32)
    if split:
        drawn = drawn * block_scale(rng, dims, split, -0.22, 0.18)
    return jnp.clip(strengthened(drawn, jax.random.fold_in(rng, 3), *heavy), -most, most).astype(held_as)


def setup_inputs(seed: int = 0) -> dict:
    key_list = jax.random.split(jax.random.key(seed), 10)
    return {
        "inputs": centred(key_list[0], (MICRO, TOKENS, D), 1.0, 6.0, ((1, 4),)),
        "out_grads": centred(key_list[1], (MICRO, TOKENS, D), 1.0, 6.0, ((1, 4),)),
        "norm_gain": jnp.clip(1.0 + 0.18 * jax.random.normal(key_list[2], (LAYERS, D), jnp.float32), 0.1, 1.9),
        "up_weight": centred(key_list[3], (LAYERS, D, FF), D ** -0.5, 0.21875, ((0, 4), (2, 2))),
        "down_weight": centred(key_list[4], (LAYERS, FF, D), FF ** -0.5, 0.109375, ((0, 4), (1, 2))),
        "prior_up_grad": heavy_noise(key_list[5], (N_DP, LAYERS, D, FF), 1.0, 6.0, ((0, 4), (1, 4), (3, 2)), (0, 2, 4, 2.0)),
        "prior_down_grad": heavy_noise(key_list[6], (N_DP, LAYERS, FF, D), 1.0, 6.0, ((0, 4), (1, 4), (2, 2)), (0, 2, 4, 2.0)),
        "master_up": centred(key_list[7], (LAYERS, D, FF), 0.05, 0.3, ((0, 4), (1, 4), (2, 2)), jnp.float32),
        "master_down": centred(key_list[8], (LAYERS, FF, D), 0.05, 0.3, ((0, 4), (1, 8)), jnp.float32),
    }


eps_norm = 1e-05
gelu_coef = 0.7978845608028654
learning_rate = 0.05

def gelu_tanh(value):
    inner = jnp.tanh(gelu_coef * (value + 0.044715 * value * value * value))
    return 0.5 * value * (1.0 + inner)

def gelu_slope(value):
    inner = jnp.tanh(gelu_coef * (value + 0.044715 * value * value * value))
    return 0.5 * (1.0 + inner) + 0.5 * value * (1.0 - inner * inner) * gelu_coef * (1.0 + 3.0 * 0.044715 * value * value)

def apply_norm(layer_entry_input, gain_vector):
    values = layer_entry_input.astype(jnp.float32)
    center = lax.optimization_barrier(jnp.mean(values, axis=-1, keepdims=True))
    centered_rows = values - center
    spread = lax.optimization_barrier(jnp.mean(centered_rows * centered_rows, axis=-1, keepdims=True))
    inverse_scale = lax.rsqrt(spread + eps_norm)
    standardized_input = centered_rows * inverse_scale
    return ((standardized_input * gain_vector).astype(jnp.bfloat16), standardized_input, inverse_scale)

def layer_forward(layer_entry_input, gain_vector, w_up, w_down):
    normalized_rows, standardized_input, inverse_scale = apply_norm(layer_entry_input, gain_vector)
    upper = jnp.dot(normalized_rows, w_up, preferred_element_type=jnp.float32)
    active = gelu_tanh(upper).astype(jnp.bfloat16)
    mixed = jnp.dot(active, w_down, preferred_element_type=jnp.float32)
    return (layer_entry_input.astype(jnp.float32) + mixed).astype(jnp.bfloat16)

def layer_backward(layer_entry_input, upstream_gradient, gain_vector, w_up, w_down):
    normalized_rows, standardized_input, inverse_scale = apply_norm(layer_entry_input, gain_vector)
    upper = jnp.dot(normalized_rows, w_up, preferred_element_type=jnp.float32)
    grad_act = jnp.dot(upstream_gradient, w_down.T, preferred_element_type=jnp.float32)
    grad_up = (grad_act * gelu_slope(upper)).astype(jnp.bfloat16)
    normalized_gradient = jnp.dot(grad_up, w_up.T, preferred_element_type=jnp.float32)
    rescaled_rows = normalized_gradient * gain_vector
    leading_operand = lax.optimization_barrier(jnp.mean(rescaled_rows, axis=-1, keepdims=True))
    trailing_operand = lax.optimization_barrier(jnp.mean(rescaled_rows * standardized_input, axis=-1, keepdims=True))
    final_output = upstream_gradient.astype(jnp.float32) + inverse_scale * (rescaled_rows - leading_operand - standardized_input * trailing_operand)
    return final_output.astype(jnp.bfloat16)

def reference(inputs, out_grads, norm_gain, up_weight, down_weight, prior_up_grad, prior_down_grad, master_up, master_down):
    outputs_all = []
    stored_inputs = []
    for layer in range(LAYERS):
        outputs_row = []
        inputs_row = []
        for micro in range(MICRO):
            current = inputs[micro] if layer == 0 else outputs_all[layer - 1][micro]
            inputs_row.append(current)
            outputs_row.append(layer_forward(current, norm_gain[layer], up_weight[layer], down_weight[layer]))
        outputs_all.append(outputs_row)
        stored_inputs.append(inputs_row)
    grads_all = [None] * LAYERS
    for layer in range(LAYERS - 1, -1, -1):
        grads_row = []
        for micro in range(MICRO):
            upstream_gradient = out_grads[micro] if layer == LAYERS - 1 else grads_all[layer + 1][micro]
            grads_row.append(layer_backward(stored_inputs[layer][micro], upstream_gradient, norm_gain[layer], up_weight[layer], down_weight[layer]))
        grads_all[layer] = grads_row
    layer_outputs = jnp.stack([jnp.stack(row) for row in outputs_all])
    input_grads = jnp.stack([jnp.stack(row) for row in grads_all])
    up_total = lax.optimization_barrier(jnp.sum(prior_up_grad.astype(jnp.float32), axis=0))
    down_total = lax.optimization_barrier(jnp.sum(prior_down_grad.astype(jnp.float32), axis=0))
    new_up = master_up - learning_rate * up_total
    new_down = master_down - learning_rate * down_total
    return (layer_outputs, input_grads, new_up, new_down)
```

```python
import functools

import jax
import jax.numpy as jnp
from jax import lax
from jax.experimental import pallas as pl
from jax.experimental.pallas import tpu as pltpu
from jax.sharding import PartitionSpec as P

eps_norm = 1e-05
gelu_coef = 0.7978845608028654
learning_rate = 0.05
MESH = pl.DeviceIdType.MESH
NT = (((1,), (1,)), ((), ()))


def flipped(index, bit):
    return index + bit - 2 * bit * (lax.rem(index // bit, 2))


def row_step(rows):
    for step in (64, 32, 16):
        if rows % step == 0:
            return step
    return rows


def subsets(bits):
    if not bits:
        return [0]
    rest = subsets(bits[1:])
    return [bits[0] + r for r in rest] + rest


class Halving:
    def __init__(self, bits, source, acc, recv, total, load_sem, send_sem, recv_sem, me):
        self.bits, self.source, self.acc, self.recv, self.total = bits, source, acc, recv, total
        self.load_sem, self.send_sem, self.recv_sem, self.me = load_sem, send_sem, recv_sem, me
        self.kept = subsets(bits[1:])
        self.slots = [(p, q) for p in range(len(bits)) for q in subsets(bits[p + 1 :])]

    def block(self, rel):
        index = self.me
        for bit in self.bits:
            if rel & bit:
                index = flipped(index, bit)
        return index

    def copy(self, slot):
        p, q = self.slots[slot]
        rel = q + self.bits[p]
        src = self.source.at[self.block(rel)] if p == 0 else self.acc.at[self.kept.index(rel)]
        return pltpu.make_async_remote_copy(
            src_ref=src,
            dst_ref=self.recv.at[slot],
            send_sem=self.send_sem.at[slot],
            recv_sem=self.recv_sem.at[slot],
            device_id={"dp": flipped(self.me, self.bits[p])},
            device_id_type=MESH,
        )

    def load(self, k):
        return pltpu.make_async_copy(
            self.source.at[self.block(self.kept[k])], self.acc.at[k], self.load_sem.at[k]
        )

    def begin(self):
        for slot, (p, _) in enumerate(self.slots):
            if p == 0:
                self.copy(slot).start()
        for k in range(len(self.kept)):
            self.load(k).start()

    def event(self, slot):
        p, q = self.slots[slot]
        k = self.kept.index(q)
        if p == 0:
            self.load(k).wait()
        self.copy(slot).wait_recv()
        last = p == len(self.bits) - 1
        rows = self.acc.shape[1]
        step = row_step(rows)

        def body(i):
            at = pl.ds(pl.multiple_of(i * step, step), step)
            summed = self.acc[k, at, :].astype(jnp.float32) + self.recv[slot, at, :].astype(jnp.float32)
            if last:
                self.total[at, :] = summed
            else:
                self.acc[k, at, :] = summed.astype(jnp.bfloat16)

        if rows == step:
            summed = self.acc[k].astype(jnp.float32) + self.recv[slot].astype(jnp.float32)
            if last:
                self.total[...] = summed
            else:
                self.acc[k] = summed.astype(jnp.bfloat16)
        else:
            pl.loop(0, rows // step)(body)
        if not last and q & self.bits[p + 1]:
            self.copy(self.slots.index((p + 1, q - self.bits[p + 1]))).start()

    def finish(self):
        for slot in range(len(self.slots)):
            self.copy(slot).wait_send()


def window_kernel(
    ns, n, nt, chunk,
    x_hbm, g_hbm, gain_ref, up_hbm, down_hbm, pu_hbm, pd_hbm,
    outs_hbm, grads_hbm, tu_ref, td_ref,
    up_v, down_v, xin, gin, ybuf, zbuf, act, slope, xhat, rstd,
    acc_u, acc_d, recv_u, recv_d,
    wl_sem, ws_sem, wr_sem, il_sem, hs_sem, hr_sem, ol_sem, os_sem, or_sem,
    rl_sem, rs_sem, rr_sem,
):
    sec = lax.axis_index("section")
    me = lax.axis_index("dp")
    ten = lax.axis_index("tensor")
    micro, rows = xin.shape[0], xin.shape[1]
    hid = up_v.shape[2]
    bits = [1 << b for b in range(n.bit_length() - 1)]
    my_rows = pl.ds(pl.multiple_of(ten * rows, rows), rows)
    peers = [lax.rem(ten + k, nt) for k in range(1, nt)]
    first, final = sec == 0, sec == ns - 1

    barrier = pltpu.get_barrier_semaphore()
    for peer in peers:
        pl.semaphore_signal(barrier, inc=1, device_id={"tensor": peer}, device_id_type=MESH)
    for bit in bits:
        pl.semaphore_signal(barrier, inc=1, device_id={"dp": flipped(me, bit)}, device_id_type=MESH)

    @pl.when(sec > 0)
    def _():
        pl.semaphore_signal(barrier, inc=1, device_id={"section": sec - 1}, device_id_type=MESH)

    @pl.when(sec < ns - 1)
    def _():
        pl.semaphore_signal(barrier, inc=1, device_id={"section": sec + 1}, device_id_type=MESH)

    own_w = [
        pltpu.make_async_copy(up_hbm, up_v.at[0], wl_sem.at[0]),
        pltpu.make_async_copy(down_hbm, down_v.at[0], wl_sem.at[1]),
    ]
    x_local = [pltpu.make_async_copy(x_hbm.at[m, my_rows, :], xin.at[m], il_sem.at[0, m]) for m in range(micro)]
    g_local = [pltpu.make_async_copy(g_hbm.at[m, my_rows, :], gin.at[m], il_sem.at[1, m]) for m in range(micro)]

    @pl.when(first)
    def _():
        for c in x_local:
            c.start()

    for c in own_w:
        c.start()

    @pl.when(final)
    def _():
        for c in g_local:
            c.start()

    ends = sec // max(ns - 1, 1) + (ns - 1 - sec) // max(ns - 1, 1) if ns > 1 else 2
    pl.semaphore_wait(barrier, len(peers) + len(bits) + 2 - ends)

    def w_copy(which, k):
        src, dst = ((up_hbm, up_v), (down_hbm, down_v))[which]
        return pltpu.make_async_remote_copy(
            src_ref=src,
            dst_ref=dst.at[k],
            send_sem=ws_sem.at[which, k - 1],
            recv_sem=wr_sem.at[which, k - 1],
            device_id={"tensor": peers[k - 1]},
            device_id_type=MESH,
        )

    for which in range(2):
        for k in range(1, nt):
            w_copy(which, k).start()

    streams = (
        Halving(bits, pu_hbm, acc_u, recv_u, tu_ref, rl_sem.at[0], rs_sem.at[0], rr_sem.at[0], me),
        Halving(bits[::-1], pd_hbm, acc_d, recv_d, td_ref, rl_sem.at[1], rs_sem.at[1], rr_sem.at[1], me),
    )
    for stream in streams:
        stream.begin()

    def hop(back, m):
        return pltpu.make_async_remote_copy(
            src_ref=(zbuf if back else ybuf).at[m],
            dst_ref=(gin if back else xin).at[m],
            send_sem=hs_sem.at[back, m],
            recv_sem=hr_sem.at[back, m],
            device_id={"section": sec - 1 if back else sec + 1},
            device_id_type=MESH,
        )

    def out_local(back, m):
        src, dst = ((ybuf, outs_hbm), (zbuf, grads_hbm))[back]
        return pltpu.make_async_copy(src.at[m], dst.at[m, my_rows, :], ol_sem.at[back, m])

    def out_remote(back, m, k):
        src, dst = ((ybuf, outs_hbm), (zbuf, grads_hbm))[back]
        return pltpu.make_async_remote_copy(
            src_ref=src.at[m],
            dst_ref=dst.at[m, my_rows, :],
            send_sem=os_sem.at[back, m, k - 1],
            recv_sem=or_sem.at[back, m, k - 1],
            device_id={"tensor": peers[k - 1]},
            device_id_type=MESH,
        )

    def give(back, m):
        out_local(back, m).start()
        for k in range(1, nt):
            out_remote(back, m, k).start()

    gain = gain_ref[...]
    cuts = [slice(c, c + chunk) for c in range(0, hid, chunk)]

    for m in range(micro):
        @pl.when(first)
        def _():
            x_local[m].wait()

        @pl.when(sec > 0)
        def _():
            hop(0, m).wait_recv()

        values = xin[m].astype(jnp.float32)
        center = jnp.mean(values, axis=-1, keepdims=True)
        centered = values - center
        spread = jnp.mean(centered * centered, axis=-1, keepdims=True)
        scale = lax.rsqrt(spread + eps_norm)
        standard = centered * scale
        xhat[m] = standard
        rstd[m] = jnp.broadcast_to(scale, rstd.shape[1:])
        normed = (standard * gain).astype(jnp.bfloat16)
        for k in range(nt):
            if m == 0:
                if k == 0:
                    own_w[0].wait()
                else:
                    w_copy(0, k).wait_recv()
            for cut in cuts:
                u = jnp.dot(normed, up_v[k, :, cut], preferred_element_type=jnp.float32)
                t = jnp.tanh(gelu_coef * (u + 0.044715 * u * u * u))
                act[k, :, cut] = (0.5 * u * (1.0 + t)).astype(jnp.bfloat16)
                slope[m, k, :, cut] = 0.5 * (1.0 + t) + 0.5 * u * (1.0 - t * t) * gelu_coef * (
                    1.0 + 3.0 * 0.044715 * u * u
                )
        mixed = None
        for k in range(nt):
            if m == 0:
                if k == 0:
                    own_w[1].wait()
                else:
                    w_copy(1, k).wait_recv()
            term = jnp.dot(act[k], down_v[k], preferred_element_type=jnp.float32)
            mixed = term if mixed is None else mixed + term
        ybuf[m] = (xin[m].astype(jnp.float32) + mixed).astype(jnp.bfloat16)

        @pl.when(sec < ns - 1)
        def _():
            hop(0, m).start()

        give(0, m)

    count = len(streams[0].slots)
    early = max(1, count // 3)
    middle = max(early, count - 1)
    for slot in range(early):
        for stream in streams:
            stream.event(slot)

    @pl.when(sec < ns - 2)
    def _():
        for slot in range(early, middle):
            for stream in streams:
                stream.event(slot)

    for m in range(micro):
        @pl.when(final)
        def _():
            g_local[m].wait()

        @pl.when(sec < ns - 1)
        def _():
            hop(1, m).wait_recv()

        g = gin[m]
        for k in range(nt):
            for cut in cuts:
                ga = lax.dot_general(g, down_v[k, cut, :], NT, preferred_element_type=jnp.float32)
                act[k, :, cut] = (ga * slope[m, k, :, cut]).astype(jnp.bfloat16)
        gn = None
        for k in range(nt):
            term = lax.dot_general(act[k], up_v[k], NT, preferred_element_type=jnp.float32)
            gn = term if gn is None else gn + term
        standard = xhat[m]
        dn = gn * gain
        lead = jnp.mean(dn, axis=-1, keepdims=True)
        trail = jnp.mean(dn * standard, axis=-1, keepdims=True)
        zbuf[m] = (
            gin[m].astype(jnp.float32) + rstd[m][:, :1] * (dn - lead - standard * trail)
        ).astype(jnp.bfloat16)

        @pl.when(sec > 0)
        def _():
            hop(1, m).start()

        give(1, m)

    @pl.when(sec >= ns - 2)
    def _():
        for slot in range(early, middle):
            for stream in streams:
                stream.event(slot)

    for slot in range(middle, count):
        for stream in streams:
            stream.event(slot)

    for stream in streams:
        stream.finish()
    for which in range(2):
        for k in range(1, nt):
            w_copy(which, k).wait_send()
    for m in range(micro):
        @pl.when(sec < ns - 1)
        def _():
            hop(0, m).wait_send()

        @pl.when(sec > 0)
        def _():
            hop(1, m).wait_send()

        for back in range(2):
            out_local(back, m).wait()
            for k in range(1, nt):
                out_remote(back, m, k).wait_send()
                out_remote(back, m, k).wait_recv()


def local(
    ns, n, nt,
    inputs, out_grads, norm_gain, up_weight, down_weight,
    prior_up_grad, prior_down_grad, master_up, master_down,
):
    micro, tokens, d = inputs.shape
    rows = tokens // nt
    hid = up_weight.shape[2]
    chunk = next((c for c in (512, 256, 128) if hid % c == 0), hid)
    pu = prior_up_grad.reshape(n, d // n, hid)
    pd = prior_down_grad.reshape(n, hid // n, d)
    bf, f32 = jnp.bfloat16, jnp.float32
    vm, dma = pltpu.VMEM, pltpu.SemaphoreType.DMA
    k = max(nt - 1, 1)
    anywhere = pl.BlockSpec(memory_space=pl.ANY)
    inside = pl.BlockSpec(memory_space=pltpu.VMEM)
    macs = micro * rows * d * hid * nt * 4
    outs, grads, total_up, total_down = pl.pallas_call(
        functools.partial(window_kernel, ns, n, nt, chunk),
        out_shape=(
            jax.ShapeDtypeStruct((micro, tokens, d), bf),
            jax.ShapeDtypeStruct((micro, tokens, d), bf),
            jax.ShapeDtypeStruct((d // n, hid), f32),
            jax.ShapeDtypeStruct((hid // n, d), f32),
        ),
        in_specs=[anywhere, anywhere, inside] + [anywhere] * 4,
        out_specs=(anywhere, anywhere, inside, inside),
        scratch_shapes=[
            vm((nt, d, hid), bf),
            vm((nt, hid, d), bf),
            vm((micro, rows, d), bf),
            vm((micro, rows, d), bf),
            vm((micro, rows, d), bf),
            vm((micro, rows, d), bf),
            vm((nt, rows, hid), bf),
            vm((micro, nt, rows, hid), f32),
            vm((micro, rows, d), f32),
            vm((micro, rows, 128), f32),
            vm((n // 2, d // n, hid), bf),
            vm((n // 2, hid // n, d), bf),
            vm((n - 1, d // n, hid), bf),
            vm((n - 1, hid // n, d), bf),
            dma((2,)), dma((2, k)), dma((2, k)),
            dma((2, micro)), dma((2, micro)), dma((2, micro)),
            dma((2, micro)), dma((2, micro, k)), dma((2, micro, k)),
            dma((2, n // 2)), dma((2, n - 1)), dma((2, n - 1)),
        ],
        compiler_params=pltpu.CompilerParams(
            collective_id=0, has_side_effects=True, vmem_limit_bytes=48 * 1024 * 1024
        ),
        cost_estimate=pl.CostEstimate(flops=2 * macs, bytes_accessed=4 * hid * d * 4, transcendentals=micro * rows * hid * nt),
        name="window",
    )(inputs, out_grads, norm_gain, up_weight[0], down_weight[0], pu, pd)
    new_up = master_up[0] - learning_rate * total_up
    new_down = master_down[0] - learning_rate * total_down
    return (outs[None], grads[None], new_up[None], new_down[None])


def solution(mesh):
    placed = (
        P(None, "dp", None),
        P(None, "dp", None),
        P("section", None),
        P("section", None, "tensor"),
        P("section", "tensor", None),
        P("dp", "section", None, "tensor"),
        P("dp", "section", "tensor", None),
        P("section", "dp", "tensor"),
        P("section", ("tensor", "dp"), None),
    )
    sizes = (mesh.shape["section"], mesh.shape["dp"], mesh.shape["tensor"])
    return jax.shard_map(
        functools.partial(local, *sizes),
        mesh=mesh,
        in_specs=placed,
        out_specs=(
            P("section", None, "dp", None),
            P("section", None, "dp", None),
            P("section", "dp", "tensor"),
            P("section", ("tensor", "dp"), None),
        ),
        check_vma=False,
    )
```

```python
import functools

import jax
import jax.numpy as jnp
from jax import lax
from jax.experimental import pallas as pl
from jax.experimental.pallas import tpu as pltpu
from jax.sharding import PartitionSpec as P

eps_norm = 1e-05
gelu_coef = 0.7978845608028654
learning_rate = 0.05
MESH = pl.DeviceIdType.MESH
NT = (((1,), (1,)), ((), ()))


def flipped(index, bit):
    return index + bit - 2 * bit * (lax.rem(index // bit, 2))


def row_step(rows):
    for step in (64, 32, 16):
        if rows % step == 0:
            return step
    return rows


def subsets(bits):
    if not bits:
        return [0]
    rest = subsets(bits[1:])
    return [bits[0] + r for r in rest] + rest


class Halving:
    def __init__(self, bits, source, acc, recv, master, total, load_sem, send_sem, recv_sem, me):
        self.bits, self.source, self.acc, self.recv, self.total = bits, source, acc, recv, total
        self.master = master
        self.load_sem, self.send_sem, self.recv_sem, self.me = load_sem, send_sem, recv_sem, me
        self.kept = subsets(bits[1:])
        self.slots = [(p, q) for p in range(len(bits)) for q in subsets(bits[p + 1 :])]

    def block(self, rel):
        index = self.me
        for bit in self.bits:
            if rel & bit:
                index = flipped(index, bit)
        return index

    def copy(self, slot):
        p, q = self.slots[slot]
        rel = q + self.bits[p]
        src = self.source.at[self.block(rel)] if p == 0 else self.acc.at[self.kept.index(rel)]
        return pltpu.make_async_remote_copy(
            src_ref=src,
            dst_ref=self.recv.at[slot],
            send_sem=self.send_sem.at[slot],
            recv_sem=self.recv_sem.at[slot],
            device_id={"dp": flipped(self.me, self.bits[p])},
            device_id_type=MESH,
        )

    def load(self, k):
        return pltpu.make_async_copy(
            self.source.at[self.block(self.kept[k])], self.acc.at[k], self.load_sem.at[k]
        )

    def begin(self):
        for slot, (p, _) in enumerate(self.slots):
            if p == 0:
                self.copy(slot).start()
        for k in range(len(self.kept)):
            self.load(k).start()

    def event(self, slot):
        p, q = self.slots[slot]
        k = self.kept.index(q)
        if p == 0:
            self.load(k).wait()
        self.copy(slot).wait_recv()
        last = p == len(self.bits) - 1
        rows = self.acc.shape[1]
        step = row_step(rows)

        def body(i):
            at = pl.ds(pl.multiple_of(i * step, step), step)
            summed = self.acc[k, at, :].astype(jnp.float32) + self.recv[slot, at, :].astype(jnp.float32)
            if last:
                self.total[at, :] = self.master[at, :] - learning_rate * summed
            else:
                self.acc[k, at, :] = summed.astype(jnp.bfloat16)

        if rows == step:
            summed = self.acc[k].astype(jnp.float32) + self.recv[slot].astype(jnp.float32)
            if last:
                self.total[...] = self.master[...] - learning_rate * summed
            else:
                self.acc[k] = summed.astype(jnp.bfloat16)
        else:
            pl.loop(0, rows // step)(body)
        if not last and q & self.bits[p + 1]:
            self.copy(self.slots.index((p + 1, q - self.bits[p + 1]))).start()

    def finish(self):
        for slot in range(len(self.slots)):
            self.copy(slot).wait_send()


def window_kernel(
    ns, n, nt, chunk,
    x_hbm, g_hbm, gain_hbm, up_hbm, down_hbm, pu_hbm, pd_hbm, mu_hbm, md_hbm,
    outs_hbm, grads_hbm, tu_ref, td_ref,
    gain_ref, up_v, down_v, up_t, down_t, master_u, master_d, xall, pall, psend, precv, xin, gin, ybuf, zbuf, act, wide, slope, xhat, rstd,
    acc_u, acc_d, recv_u, recv_d,
    wl_sem, ml_sem, ps_sem, pr_sem, ws_sem, wr_sem, il_sem, hs_sem, hr_sem, ol_sem, os_sem, or_sem,
    rl_sem, rs_sem, rr_sem,
):
    sec = lax.axis_index("section")
    me = lax.axis_index("dp")
    ten = lax.axis_index("tensor")
    micro, rows = xin.shape[0], xin.shape[1]
    hid = up_v.shape[2]
    bits = [1 << b for b in range(n.bit_length() - 1)]
    my_rows = pl.ds(pl.multiple_of(ten * rows, rows), rows)
    peers = [lax.rem(ten + k, nt) for k in range(1, nt)]
    first, final = sec == 0, sec == ns - 1

    barrier = pltpu.get_barrier_semaphore()
    for peer in peers:
        pl.semaphore_signal(barrier, inc=1, device_id={"tensor": peer}, device_id_type=MESH)
    for bit in bits:
        pl.semaphore_signal(barrier, inc=1, device_id={"dp": flipped(me, bit)}, device_id_type=MESH)

    @pl.when(sec > 0)
    def _():
        pl.semaphore_signal(barrier, inc=1, device_id={"section": sec - 1}, device_id_type=MESH)

    @pl.when(sec < ns - 1)
    def _():
        pl.semaphore_signal(barrier, inc=1, device_id={"section": sec + 1}, device_id_type=MESH)

    own_w = [
        pltpu.make_async_copy(up_hbm, up_v.at[0], wl_sem.at[0]),
        pltpu.make_async_copy(down_hbm, down_v.at[0], wl_sem.at[1]),
    ]
    x_local = [pltpu.make_async_copy(x_hbm.at[m, my_rows, :], xin.at[m], il_sem.at[0, m]) for m in range(micro)]
    g_local = [pltpu.make_async_copy(g_hbm.at[m, my_rows, :], gin.at[m], il_sem.at[1, m]) for m in range(micro)]

    x_whole = [pltpu.make_async_copy(x_hbm.at[m], xall.at[m], il_sem.at[2, m]) for m in range(micro)]
    own_m = [
        pltpu.make_async_copy(mu_hbm, master_u, ml_sem.at[0]),
        pltpu.make_async_copy(md_hbm, master_d, ml_sem.at[1]),
    ]
    gain_load = pltpu.make_async_copy(gain_hbm, gain_ref, ml_sem.at[2])
    gain_load.start()

    @pl.when(first)
    def _():
        for c in x_whole:
            c.start()
        for c in x_local:
            c.start()

    for c in own_w:
        c.start()

    @pl.when(final)
    def _():
        for c in g_local:
            c.start()

    ends = sec // max(ns - 1, 1) + (ns - 1 - sec) // max(ns - 1, 1) if ns > 1 else 2
    pl.semaphore_wait(barrier, len(peers) + len(bits) + 2 - ends)

    def w_copy(which, k):
        src, dst = ((up_hbm, up_v), (down_hbm, down_v))[which]
        return pltpu.make_async_remote_copy(
            src_ref=src,
            dst_ref=dst.at[k],
            send_sem=ws_sem.at[which, k - 1],
            recv_sem=wr_sem.at[which, k - 1],
            device_id={"tensor": peers[k - 1]},
            device_id_type=MESH,
        )

    def trade():
        for which in range(2):
            for k in range(1, nt):
                w_copy(which, k).start()

    @pl.when(sec > 0)
    def _():
        trade()

    streams = (
        Halving(bits, pu_hbm, acc_u, recv_u, master_u, tu_ref, rl_sem.at[0], rs_sem.at[0], rr_sem.at[0], me),
        Halving(bits[::-1], pd_hbm, acc_d, recv_d, master_d, td_ref, rl_sem.at[1], rs_sem.at[1], rr_sem.at[1], me),
    )
    for stream in streams:
        stream.begin()
    for c in own_m:
        c.start()

    def hop(back, m):
        return pltpu.make_async_remote_copy(
            src_ref=(zbuf if back else ybuf).at[m],
            dst_ref=(gin if back else xin).at[m],
            send_sem=hs_sem.at[back, m],
            recv_sem=hr_sem.at[back, m],
            device_id={"section": sec - 1 if back else sec + 1},
            device_id_type=MESH,
        )

    def out_local(back, m):
        src, dst = ((ybuf, outs_hbm), (zbuf, grads_hbm))[back]
        return pltpu.make_async_copy(src.at[m], dst.at[m, my_rows, :], ol_sem.at[back, m])

    def out_remote(back, m, k):
        src, dst = ((ybuf, outs_hbm), (zbuf, grads_hbm))[back]
        return pltpu.make_async_remote_copy(
            src_ref=src.at[m],
            dst_ref=dst.at[m, my_rows, :],
            send_sem=os_sem.at[back, m, k - 1],
            recv_sem=or_sem.at[back, m, k - 1],
            device_id={"tensor": peers[k - 1]},
            device_id_type=MESH,
        )

    def give(back, m):
        out_local(back, m).start()
        for k in range(1, nt):
            out_remote(back, m, k).start()

    gain_load.wait()
    gain = gain_ref[...]
    cuts = [slice(c, c + chunk) for c in range(0, hid, chunk)]

    def normalized(values):
        center = jnp.mean(values, axis=-1, keepdims=True)
        centered = values - center
        spread = jnp.mean(centered * centered, axis=-1, keepdims=True)
        scale = lax.rsqrt(spread + eps_norm)
        return centered * scale, scale

    def part(m, k):
        return pltpu.make_async_remote_copy(
            src_ref=psend.at[m, k - 1],
            dst_ref=precv.at[m, k - 1],
            send_sem=ps_sem.at[m, k - 1],
            recv_sem=pr_sem.at[m, k - 1],
            device_id={"tensor": peers[k - 1]},
            device_id_type=MESH,
        )

    def front(m):
        standard, scale = normalized(xin[m].astype(jnp.float32))
        xhat[m] = standard
        rstd[m] = jnp.broadcast_to(scale, rstd.shape[1:])
        normed = (standard * gain).astype(jnp.bfloat16)
        for k in range(nt):
            for cut in cuts:
                u = jnp.dot(normed, up_v[k, :, cut], preferred_element_type=jnp.float32)
                t = jnp.tanh(gelu_coef * (u + 0.044715 * u * u * u))
                act[k, :, cut] = (0.5 * u * (1.0 + t)).astype(jnp.bfloat16)
                slope[m, k, :, cut] = 0.5 * (1.0 + t) + 0.5 * u * (1.0 - t * t) * gelu_coef * (
                    1.0 + 3.0 * 0.044715 * u * u
                )

    def weights_here(own):
        if own:
            for c in own_w:
                c.wait()
        for which in range(2):
            for k in range(1, nt):
                w_copy(which, k).wait_recv()

    tile = next((c for c in (256, 128) if hid % c == 0), hid)

    def turn():
        for k in range(nt):
            @pl.loop(0, hid // tile)
            def _(i):
                at = pl.ds(pl.multiple_of(i * tile, tile), tile)
                down_t[k, :, at] = down_v[k, at, :].T
                up_t[k, at, :] = up_v[k, :, at].T

    count = len(streams[0].slots)

    def events(start, stop):
        for slot in range(start, stop):
            for stream in streams:
                if slot == count - 1:
                    own_m[streams.index(stream)].wait()
                stream.event(slot)

    @pl.when(first)
    def _():
        for m in range(micro):
            x_whole[m].wait()
            if m == 0:
                own_w[0].wait()
            standard, _ = normalized(xall[m].astype(jnp.float32))
            normed = (standard * gain).astype(jnp.bfloat16)
            for cut in cuts:
                u = jnp.dot(normed, up_v[0, :, cut], preferred_element_type=jnp.float32)
                t = jnp.tanh(gelu_coef * (u + 0.044715 * u * u * u))
                wide[:, cut] = (0.5 * u * (1.0 + t)).astype(jnp.bfloat16)
            if m == 0:
                own_w[1].wait()
            pall[m] = jnp.dot(wide[...], down_v[0], preferred_element_type=jnp.float32)
            for k in range(1, nt):
                at = pl.ds(pl.multiple_of(peers[k - 1] * rows, rows), rows)
                psend[m, k - 1] = pall[m, at, :].astype(jnp.bfloat16)
                part(m, k).start()
        for m in range(micro):
            x_local[m].wait()
            mixed = pall[m, my_rows, :]
            for k in range(1, nt):
                part(m, k).wait_recv()
                mixed = mixed + precv[m, k - 1].astype(jnp.float32)
            ybuf[m] = (xin[m].astype(jnp.float32) + mixed).astype(jnp.bfloat16)

            @pl.when(sec < ns - 1)
            def _():
                hop(0, m).start()

            give(0, m)
        trade()
        weights_here(False)
        for m in range(micro):
            front(m)
            for k in range(1, nt):
                part(m, k).wait_send()

    @pl.when(sec > 0)
    def _():
        weights_here(True)

    @pl.when(sec >= 2)
    def _():
        turn()

    @pl.when(final)
    def _():
        events(0, 1)

    @pl.when(sec > 0)
    def _():
        for m in range(micro):
            hop(0, m).wait_recv()
            front(m)
            mixed = None
            for k in range(nt):
                term = jnp.dot(act[k], down_v[k], preferred_element_type=jnp.float32)
                mixed = term if mixed is None else mixed + term
            ybuf[m] = (xin[m].astype(jnp.float32) + mixed).astype(jnp.bfloat16)

            @pl.when(sec < ns - 1)
            def _():
                hop(0, m).start()

            give(0, m)

    @pl.when(sec < 2)
    def _():
        turn()

    @pl.when(sec < ns - 1)
    def _():
        events(0, count)

    for m in range(micro):
        @pl.when(final)
        def _():
            g_local[m].wait()

        @pl.when(sec < ns - 1)
        def _():
            hop(1, m).wait_recv()

        g = gin[m]
        for k in range(nt):
            for cut in cuts:
                ga = jnp.dot(g, down_t[k, :, cut], preferred_element_type=jnp.float32)
                act[k, :, cut] = (ga * slope[m, k, :, cut]).astype(jnp.bfloat16)
        gn = None
        for k in range(nt):
            term = jnp.dot(act[k], up_t[k], preferred_element_type=jnp.float32)
            gn = term if gn is None else gn + term
        standard = xhat[m]
        dn = gn * gain
        lead = jnp.mean(dn, axis=-1, keepdims=True)
        trail = jnp.mean(dn * standard, axis=-1, keepdims=True)
        zbuf[m] = (
            gin[m].astype(jnp.float32) + rstd[m][:, :1] * (dn - lead - standard * trail)
        ).astype(jnp.bfloat16)

        @pl.when(sec > 0)
        def _():
            hop(1, m).start()

        give(1, m)

    @pl.when(final)
    def _():
        events(1, count)

    for stream in streams:
        stream.finish()
    for which in range(2):
        for k in range(1, nt):
            w_copy(which, k).wait_send()
    for m in range(micro):
        @pl.when(sec < ns - 1)
        def _():
            hop(0, m).wait_send()

        @pl.when(sec > 0)
        def _():
            hop(1, m).wait_send()

        for back in range(2):
            out_local(back, m).wait()
            for k in range(1, nt):
                out_remote(back, m, k).wait_send()
                out_remote(back, m, k).wait_recv()


def local(
    ns, n, nt,
    inputs, out_grads, norm_gain, up_weight, down_weight,
    prior_up_grad, prior_down_grad, master_up, master_down,
):
    micro, tokens, d = inputs.shape
    rows = tokens // nt
    hid = up_weight.shape[2]
    chunk = next((c for c in (512, 256, 128) if hid % c == 0), hid)
    pu = prior_up_grad.reshape(n, d // n, hid)
    pd = prior_down_grad.reshape(n, hid // n, d)
    bf, f32 = jnp.bfloat16, jnp.float32
    vm, dma = pltpu.VMEM, pltpu.SemaphoreType.DMA
    k = max(nt - 1, 1)
    inside = pl.BlockSpec(memory_space=pltpu.VMEM)
    macs = micro * rows * d * hid * nt * 4
    anywhere = pl.BlockSpec(memory_space=pl.ANY)
    hbm = pl.BlockSpec(memory_space=pltpu.HBM)
    outs, grads, new_up, new_down = pl.pallas_call(
        functools.partial(window_kernel, ns, n, nt, chunk),
        out_shape=(
            jax.ShapeDtypeStruct((micro, tokens, d), bf),
            jax.ShapeDtypeStruct((micro, tokens, d), bf),
            jax.ShapeDtypeStruct((d // n, hid), f32),
            jax.ShapeDtypeStruct((hid // n, d), f32),
        ),
        in_specs=[hbm] * 9,
        out_specs=(anywhere, anywhere, inside, inside),
        scratch_shapes=[
            vm((1, d), f32),
            vm((nt, d, hid), bf),
            vm((nt, hid, d), bf),
            vm((nt, hid, d), bf),
            vm((nt, d, hid), bf),
            vm((d // n, hid), f32),
            vm((hid // n, d), f32),
            vm((micro, tokens, d), bf),
            vm((micro, tokens, d), f32),
            vm((micro, k, rows, d), bf),
            vm((micro, k, rows, d), bf),
            vm((micro, rows, d), bf),
            vm((micro, rows, d), bf),
            vm((micro, rows, d), bf),
            vm((micro, rows, d), bf),
            vm((nt, rows, hid), bf),
            vm((tokens, hid), bf),
            vm((micro, nt, rows, hid), f32),
            vm((micro, rows, d), f32),
            vm((micro, rows, 128), f32),
            vm((n // 2, d // n, hid), bf),
            vm((n // 2, hid // n, d), bf),
            vm((n - 1, d // n, hid), bf),
            vm((n - 1, hid // n, d), bf),
            dma((2,)), dma((3,)), dma((micro, k)), dma((micro, k)), dma((2, k)), dma((2, k)),
            dma((3, micro)), dma((2, micro)), dma((2, micro)),
            dma((2, micro)), dma((2, micro, k)), dma((2, micro, k)),
            dma((2, n // 2)), dma((2, n - 1)), dma((2, n - 1)),
        ],
        compiler_params=pltpu.CompilerParams(
            collective_id=0, has_side_effects=True, vmem_limit_bytes=46 * 1024 * 1024
        ),
        cost_estimate=pl.CostEstimate(flops=2 * macs, bytes_accessed=4 * hid * d * 4, transcendentals=micro * rows * hid * nt),
        name="window",
    )(inputs, out_grads, norm_gain, up_weight[0], down_weight[0], pu, pd, master_up[0], master_down[0])
    return (outs[None], grads[None], new_up[None], new_down[None])


def solution(mesh):
    placed = (
        P(None, "dp", None),
        P(None, "dp", None),
        P("section", None),
        P("section", None, "tensor"),
        P("section", "tensor", None),
        P("dp", "section", None, "tensor"),
        P("dp", "section", "tensor", None),
        P("section", "dp", "tensor"),
        P("section", ("tensor", "dp"), None),
    )
    sizes = (mesh.shape["section"], mesh.shape["dp"], mesh.shape["tensor"])
    return jax.shard_map(
        functools.partial(local, *sizes),
        mesh=mesh,
        in_specs=placed,
        out_specs=(
            P("section", None, "dp", None),
            P("section", None, "dp", None),
            P("section", "dp", "tensor"),
            P("section", ("tensor", "dp"), None),
        ),
        check_vma=False,
    )
```

```python
import functools

import jax
import jax.numpy as jnp
from jax import lax
from jax.experimental import pallas as pl
from jax.experimental.pallas import tpu as pltpu
from jax.sharding import PartitionSpec as P

eps_norm = 1e-05
gelu_coef = 0.7978845608028654
learning_rate = 0.05
MESH = pl.DeviceIdType.MESH
NT = (((1,), (1,)), ((), ()))


def flipped(index, bit):
    return index + bit - 2 * bit * (lax.rem(index // bit, 2))


def row_step(rows):
    for step in (64, 32, 16):
        if rows % step == 0:
            return step
    return rows


def subsets(bits):
    if not bits:
        return [0]
    rest = subsets(bits[1:])
    return [bits[0] + r for r in rest] + rest


class Halving:
    def __init__(self, bits, source, acc, recv, master, total, load_sem, send_sem, recv_sem, me):
        self.bits, self.source, self.acc, self.recv, self.total = bits, source, acc, recv, total
        self.master = master
        self.load_sem, self.send_sem, self.recv_sem, self.me = load_sem, send_sem, recv_sem, me
        self.kept = subsets(bits[1:])
        self.slots = [(p, q) for p in range(len(bits)) for q in subsets(bits[p + 1 :])]

    def block(self, rel):
        index = self.me
        for bit in self.bits:
            if rel & bit:
                index = flipped(index, bit)
        return index

    def copy(self, slot):
        p, q = self.slots[slot]
        rel = q + self.bits[p]
        src = self.source.at[self.block(rel)] if p == 0 else self.acc.at[self.kept.index(rel)]
        return pltpu.make_async_remote_copy(
            src_ref=src,
            dst_ref=self.recv.at[slot],
            send_sem=self.send_sem.at[slot],
            recv_sem=self.recv_sem.at[slot],
            device_id={"dp": flipped(self.me, self.bits[p])},
            device_id_type=MESH,
        )

    def load(self, k):
        return pltpu.make_async_copy(
            self.source.at[self.block(self.kept[k])], self.acc.at[k], self.load_sem.at[k]
        )

    def begin(self):
        for slot, (p, _) in enumerate(self.slots):
            if p == 0:
                self.copy(slot).start()

    def begin_loads(self):
        for k in range(len(self.kept)):
            self.load(k).start()

    def event(self, slot):
        p, q = self.slots[slot]
        k = self.kept.index(q)
        if p == 0:
            self.load(k).wait()
        self.copy(slot).wait_recv()
        last = p == len(self.bits) - 1
        rows = self.acc.shape[1]
        step = row_step(rows)

        def body(i):
            at = pl.ds(pl.multiple_of(i * step, step), step)
            summed = self.acc[k, at, :].astype(jnp.float32) + self.recv[slot, at, :].astype(jnp.float32)
            if last:
                self.total[at, :] = self.master[at, :] - learning_rate * summed
            else:
                self.acc[k, at, :] = summed.astype(jnp.bfloat16)

        if rows == step:
            summed = self.acc[k].astype(jnp.float32) + self.recv[slot].astype(jnp.float32)
            if last:
                self.total[...] = self.master[...] - learning_rate * summed
            else:
                self.acc[k] = summed.astype(jnp.bfloat16)
        else:
            pl.loop(0, rows // step)(body)
        if not last and q & self.bits[p + 1]:
            self.copy(self.slots.index((p + 1, q - self.bits[p + 1]))).start()

    def finish(self):
        for slot in range(len(self.slots)):
            self.copy(slot).wait_send()


def window_kernel(
    ns, n, nt, chunk,
    x_hbm, g_hbm, gain_hbm, up_hbm, down_hbm, pu_hbm, pd_hbm, mu_hbm, md_hbm,
    outs_hbm, grads_hbm, tu_ref, td_ref,
    gain_ref, up_v, down_v, up_t, down_t, master_u, master_d, xall, pall, psend, precv, xin, gin, ybuf, zbuf, act, wide, slope, xhat, rstd,
    acc_u, acc_d, recv_u, recv_d,
    wl_sem, ml_sem, ps_sem, pr_sem, ws_sem, wr_sem, il_sem, hs_sem, hr_sem, ol_sem, os_sem, or_sem,
    rl_sem, rs_sem, rr_sem,
):
    sec = lax.axis_index("section")
    me = lax.axis_index("dp")
    ten = lax.axis_index("tensor")
    micro, rows = xin.shape[0], xin.shape[1]
    hid = up_v.shape[2]
    bits = [1 << b for b in range(n.bit_length() - 1)]
    my_rows = pl.ds(pl.multiple_of(ten * rows, rows), rows)
    peers = [lax.rem(ten + k, nt) for k in range(1, nt)]
    first, final = sec == 0, sec == ns - 1

    barrier = pltpu.get_barrier_semaphore()
    for peer in peers:
        pl.semaphore_signal(barrier, inc=1, device_id={"tensor": peer}, device_id_type=MESH)
    for bit in bits:
        pl.semaphore_signal(barrier, inc=1, device_id={"dp": flipped(me, bit)}, device_id_type=MESH)

    @pl.when(sec > 0)
    def _():
        pl.semaphore_signal(barrier, inc=1, device_id={"section": sec - 1}, device_id_type=MESH)

    @pl.when(sec < ns - 1)
    def _():
        pl.semaphore_signal(barrier, inc=1, device_id={"section": sec + 1}, device_id_type=MESH)

    own_w = [
        pltpu.make_async_copy(up_hbm, up_v.at[0], wl_sem.at[0]),
        pltpu.make_async_copy(down_hbm, down_v.at[0], wl_sem.at[1]),
    ]
    x_local = [pltpu.make_async_copy(x_hbm.at[m, my_rows, :], xin.at[m], il_sem.at[0, m]) for m in range(micro)]
    g_local = [pltpu.make_async_copy(g_hbm.at[m, my_rows, :], gin.at[m], il_sem.at[1, m]) for m in range(micro)]

    x_whole = [pltpu.make_async_copy(x_hbm.at[m], xall.at[m], il_sem.at[2, m]) for m in range(micro)]
    own_m = [
        pltpu.make_async_copy(mu_hbm, master_u, ml_sem.at[0]),
        pltpu.make_async_copy(md_hbm, master_d, ml_sem.at[1]),
    ]
    gain_load = pltpu.make_async_copy(gain_hbm, gain_ref, ml_sem.at[2])
    gain_load.start()

    @pl.when(first)
    def _():
        for c in x_whole:
            c.start()
        for c in x_local:
            c.start()

    for c in own_w:
        c.start()

    @pl.when(final)
    def _():
        for c in g_local:
            c.start()

    ends = sec // max(ns - 1, 1) + (ns - 1 - sec) // max(ns - 1, 1) if ns > 1 else 2
    pl.semaphore_wait(barrier, len(peers) + len(bits) + 2 - ends)

    def w_copy(which, k):
        src, dst = ((up_hbm, up_v), (down_hbm, down_v))[which]
        return pltpu.make_async_remote_copy(
            src_ref=src,
            dst_ref=dst.at[k],
            send_sem=ws_sem.at[which, k - 1],
            recv_sem=wr_sem.at[which, k - 1],
            device_id={"tensor": peers[k - 1]},
            device_id_type=MESH,
        )

    def trade():
        for which in range(2):
            for k in range(1, nt):
                w_copy(which, k).start()

    @pl.when(sec > 0)
    def _():
        trade()

    streams = (
        Halving(bits, pu_hbm, acc_u, recv_u, master_u, tu_ref, rl_sem.at[0], rs_sem.at[0], rr_sem.at[0], me),
        Halving(bits[::-1], pd_hbm, acc_d, recv_d, master_d, td_ref, rl_sem.at[1], rs_sem.at[1], rr_sem.at[1], me),
    )
    for stream in streams:
        stream.begin()

    def loads():
        for stream in streams:
            stream.begin_loads()
        for c in own_m:
            c.start()

    @pl.when(sec > 0)
    def _():
        loads()


    def hop(back, m):
        return pltpu.make_async_remote_copy(
            src_ref=(zbuf if back else ybuf).at[m],
            dst_ref=(gin if back else xin).at[m],
            send_sem=hs_sem.at[back, m],
            recv_sem=hr_sem.at[back, m],
            device_id={"section": sec - 1 if back else sec + 1},
            device_id_type=MESH,
        )

    def out_local(back, m):
        src, dst = ((ybuf, outs_hbm), (zbuf, grads_hbm))[back]
        return pltpu.make_async_copy(src.at[m], dst.at[m, my_rows, :], ol_sem.at[back, m])

    def out_remote(back, m, k):
        src, dst = ((ybuf, outs_hbm), (zbuf, grads_hbm))[back]
        return pltpu.make_async_remote_copy(
            src_ref=src.at[m],
            dst_ref=dst.at[m, my_rows, :],
            send_sem=os_sem.at[back, m, k - 1],
            recv_sem=or_sem.at[back, m, k - 1],
            device_id={"tensor": peers[k - 1]},
            device_id_type=MESH,
        )

    def give(back, m):
        out_local(back, m).start()
        for k in range(1, nt):
            out_remote(back, m, k).start()

    gain_load.wait()
    gain = gain_ref[...]
    cuts = [slice(c, c + chunk) for c in range(0, hid, chunk)]

    def normalized(values):
        center = jnp.mean(values, axis=-1, keepdims=True)
        centered = values - center
        spread = jnp.mean(centered * centered, axis=-1, keepdims=True)
        scale = lax.rsqrt(spread + eps_norm)
        return centered * scale, scale

    def part(m, k):
        return pltpu.make_async_remote_copy(
            src_ref=psend.at[m, k - 1],
            dst_ref=precv.at[m, k - 1],
            send_sem=ps_sem.at[m, k - 1],
            recv_sem=pr_sem.at[m, k - 1],
            device_id={"tensor": peers[k - 1]},
            device_id_type=MESH,
        )

    def front(m):
        standard, scale = normalized(xin[m].astype(jnp.float32))
        xhat[m] = standard
        rstd[m] = jnp.broadcast_to(scale, rstd.shape[1:])
        normed = (standard * gain).astype(jnp.bfloat16)
        for k in range(nt):
            for cut in cuts:
                u = jnp.dot(normed, up_v[k, :, cut], preferred_element_type=jnp.float32)
                t = jnp.tanh(gelu_coef * (u + 0.044715 * u * u * u))
                act[k, :, cut] = (0.5 * u * (1.0 + t)).astype(jnp.bfloat16)
                slope[m, k, :, cut] = 0.5 * (1.0 + t) + 0.5 * u * (1.0 - t * t) * gelu_coef * (
                    1.0 + 3.0 * 0.044715 * u * u
                )

    def weights_here(own):
        if own:
            for c in own_w:
                c.wait()
        for which in range(2):
            for k in range(1, nt):
                w_copy(which, k).wait_recv()

    tile = next((c for c in (256, 128) if hid % c == 0), hid)

    def turn():
        for k in range(nt):
            @pl.loop(0, hid // tile)
            def _(i):
                at = pl.ds(pl.multiple_of(i * tile, tile), tile)
                down_t[k, :, at] = down_v[k, at, :].T
                up_t[k, at, :] = up_v[k, :, at].T

    count = len(streams[0].slots)

    def events(start, stop):
        for slot in range(start, stop):
            for stream in streams:
                if slot == count - 1:
                    own_m[streams.index(stream)].wait()
                stream.event(slot)

    @pl.when(first)
    def _():
        for m in range(micro):
            x_whole[m].wait()
            if m == 0:
                own_w[0].wait()
            standard, _ = normalized(xall[m].astype(jnp.float32))
            normed = (standard * gain).astype(jnp.bfloat16)
            for cut in cuts:
                u = jnp.dot(normed, up_v[0, :, cut], preferred_element_type=jnp.float32)
                t = jnp.tanh(gelu_coef * (u + 0.044715 * u * u * u))
                wide[:, cut] = (0.5 * u * (1.0 + t)).astype(jnp.bfloat16)
            if m == 0:
                own_w[1].wait()
            pall[m] = jnp.dot(wide[...], down_v[0], preferred_element_type=jnp.float32)
            for k in range(1, nt):
                at = pl.ds(pl.multiple_of(peers[k - 1] * rows, rows), rows)
                psend[m, k - 1] = pall[m, at, :].astype(jnp.bfloat16)
                part(m, k).start()
        for m in range(micro):
            x_local[m].wait()
            mixed = pall[m, my_rows, :]
            for k in range(1, nt):
                part(m, k).wait_recv()
                mixed = mixed + precv[m, k - 1].astype(jnp.float32)
            ybuf[m] = (xin[m].astype(jnp.float32) + mixed).astype(jnp.bfloat16)

            @pl.when(sec < ns - 1)
            def _():
                hop(0, m).start()

            give(0, m)
        trade()
        loads()
        weights_here(False)
        for m in range(micro):
            front(m)
            for k in range(1, nt):
                part(m, k).wait_send()

    @pl.when(sec > 0)
    def _():
        weights_here(True)

    @pl.when(sec >= 2)
    def _():
        turn()

    @pl.when(final)
    def _():
        events(0, 1)

    @pl.when(sec > 0)
    def _():
        for m in range(micro):
            hop(0, m).wait_recv()
            front(m)
            mixed = None
            for k in range(nt):
                term = jnp.dot(act[k], down_v[k], preferred_element_type=jnp.float32)
                mixed = term if mixed is None else mixed + term
            ybuf[m] = (xin[m].astype(jnp.float32) + mixed).astype(jnp.bfloat16)

            @pl.when(sec < ns - 1)
            def _():
                hop(0, m).start()

            give(0, m)

    @pl.when(sec < 2)
    def _():
        turn()

    @pl.when(sec < ns - 1)
    def _():
        events(0, count)

    for m in range(micro):
        @pl.when(final)
        def _():
            g_local[m].wait()

        @pl.when(sec < ns - 1)
        def _():
            hop(1, m).wait_recv()

        g = gin[m]
        for k in range(nt):
            for cut in cuts:
                ga = jnp.dot(g, down_t[k, :, cut], preferred_element_type=jnp.float32)
                act[k, :, cut] = (ga * slope[m, k, :, cut]).astype(jnp.bfloat16)
        gn = None
        for k in range(nt):
            term = jnp.dot(act[k], up_t[k], preferred_element_type=jnp.float32)
            gn = term if gn is None else gn + term
        standard = xhat[m]
        dn = gn * gain
        lead = jnp.mean(dn, axis=-1, keepdims=True)
        trail = jnp.mean(dn * standard, axis=-1, keepdims=True)
        zbuf[m] = (
            gin[m].astype(jnp.float32) + rstd[m][:, :1] * (dn - lead - standard * trail)
        ).astype(jnp.bfloat16)

        @pl.when(sec > 0)
        def _():
            hop(1, m).start()

        give(1, m)

    @pl.when(final)
    def _():
        events(1, count)

    for stream in streams:
        stream.finish()
    for which in range(2):
        for k in range(1, nt):
            w_copy(which, k).wait_send()
    for m in range(micro):
        @pl.when(sec < ns - 1)
        def _():
            hop(0, m).wait_send()

        @pl.when(sec > 0)
        def _():
            hop(1, m).wait_send()

        for back in range(2):
            out_local(back, m).wait()
            for k in range(1, nt):
                out_remote(back, m, k).wait_send()
                out_remote(back, m, k).wait_recv()


def local(
    ns, n, nt,
    inputs, out_grads, norm_gain, up_weight, down_weight,
    prior_up_grad, prior_down_grad, master_up, master_down,
):
    micro, tokens, d = inputs.shape
    rows = tokens // nt
    hid = up_weight.shape[2]
    chunk = next((c for c in (512, 256, 128) if hid % c == 0), hid)
    pu = prior_up_grad.reshape(n, d // n, hid)
    pd = prior_down_grad.reshape(n, hid // n, d)
    bf, f32 = jnp.bfloat16, jnp.float32
    vm, dma = pltpu.VMEM, pltpu.SemaphoreType.DMA
    k = max(nt - 1, 1)
    inside = pl.BlockSpec(memory_space=pltpu.VMEM)
    macs = micro * rows * d * hid * nt * 4
    anywhere = pl.BlockSpec(memory_space=pl.ANY)
    hbm = pl.BlockSpec(memory_space=pltpu.HBM)
    outs, grads, new_up, new_down = pl.pallas_call(
        functools.partial(window_kernel, ns, n, nt, chunk),
        out_shape=(
            pltpu.VMEM((micro, tokens, d), bf),
            pltpu.VMEM((micro, tokens, d), bf),
            pltpu.VMEM((d // n, hid), f32),
            pltpu.VMEM((hid // n, d), f32),
        ),
        in_specs=[hbm] * 9,
        out_specs=(anywhere, anywhere, inside, inside),
        scratch_shapes=[
            vm((1, d), f32),
            vm((nt, d, hid), bf),
            vm((nt, hid, d), bf),
            vm((nt, hid, d), bf),
            vm((nt, d, hid), bf),
            vm((d // n, hid), f32),
            vm((hid // n, d), f32),
            vm((micro, tokens, d), bf),
            vm((micro, tokens, d), f32),
            vm((micro, k, rows, d), bf),
            vm((micro, k, rows, d), bf),
            vm((micro, rows, d), bf),
            vm((micro, rows, d), bf),
            vm((micro, rows, d), bf),
            vm((micro, rows, d), bf),
            vm((nt, rows, hid), bf),
            vm((tokens, hid), bf),
            vm((micro, nt, rows, hid), f32),
            vm((micro, rows, d), f32),
            vm((micro, rows, 128), f32),
            vm((n // 2, d // n, hid), bf),
            vm((n // 2, hid // n, d), bf),
            vm((n - 1, d // n, hid), bf),
            vm((n - 1, hid // n, d), bf),
            dma((2,)), dma((3,)), dma((micro, k)), dma((micro, k)), dma((2, k)), dma((2, k)),
            dma((3, micro)), dma((2, micro)), dma((2, micro)),
            dma((2, micro)), dma((2, micro, k)), dma((2, micro, k)),
            dma((2, n // 2)), dma((2, n - 1)), dma((2, n - 1)),
        ],
        compiler_params=pltpu.CompilerParams(
            collective_id=0, has_side_effects=True, vmem_limit_bytes=54 * 1024 * 1024
        ),
        cost_estimate=pl.CostEstimate(flops=2 * macs, bytes_accessed=4 * hid * d * 4, transcendentals=micro * rows * hid * nt),
        name="window",
    )(inputs, out_grads, norm_gain, up_weight[0], down_weight[0], pu, pd, master_up[0], master_down[0])
    return (outs[None], grads[None], new_up[None], new_down[None])


def solution(mesh):
    placed = (
        P(None, "dp", None),
        P(None, "dp", None),
        P("section", None),
        P("section", None, "tensor"),
        P("section", "tensor", None),
        P("dp", "section", None, "tensor"),
        P("dp", "section", "tensor", None),
        P("section", "dp", "tensor"),
        P("section", ("tensor", "dp"), None),
    )
    sizes = (mesh.shape["section"], mesh.shape["dp"], mesh.shape["tensor"])
    return jax.shard_map(
        functools.partial(local, *sizes),
        mesh=mesh,
        in_specs=placed,
        out_specs=(
            P("section", None, "dp", None),
            P("section", None, "dp", None),
            P("section", "dp", "tensor"),
            P("section", ("tensor", "dp"), None),
        ),
        check_vma=False,
    )
```
